256 devices in a mesh: front: 4 (over x_hi, core), row: 8 (over z), col: 8 (over y, x_lo).
Axes of the slice: x: 4 (x_hi: 2, x_lo: 2; x = x_hi * 2 + x_lo), y: 4, z: 8, core: 2. Of those that a mesh axis runs over, the one named last changes fastest.
Arguments:
- front_block: float32 [4, 8192, 8192], P('front', 'row', 'col'), as said below
- child_map: int32 [4, 60], replicated, may hold values from 8 to 127, as said below
- parent_entries: float32 [16384, 16384], P(('front', 'row'), 'col'), may hold values from -2 to 2
Outputs:
- parent_front: float32 [16384, 16384], P(('front', 'row'), 'col')
The draws below stay inside these ranges and needn't reach their ends.
Inputs may be any that keep to these rules, and one draw needn't show every extreme that they name: child_map[f, s] is 2 (s + 4) or one more. Each front_block[f] is symmetric and its leading 512 x 512 block is positive definite.
All inputs are finite; a program needn't handle non-finite values.
Results may differ from the reference program's by a relative error of at most 0.0001.
Values sent between devices are 32-bit elements; how exact they have to be, the bound alone decides.
No kernel may reach another device: no remote copies, remote signals or barrier semaphores. Data moves between devices by JAX's collectives and lax.ppermute only.
A program may use at most 128 MiB of HBM per device.

```python
import math
import jax
import jax.numpy as jnp
from jax import lax

FRONT = 8192
PANEL = 512
TILE = 128
FRONTS = 4
PARENT = 16384


def draw_front_block(key, part):
    key = jax.random.fold_in(key, 1)
    noise_key, diag_key = jax.random.split(key)
    shape = (FRONTS, FRONT, FRONT)
    noise = jax.random.normal(noise_key, shape, jnp.float32)
    symmetric = (noise + jnp.swapaxes(noise, 1, 2)) * (0.25 / math.sqrt(2.0))
    diagonal = jax.random.uniform(diag_key, (FRONTS, FRONT), jnp.float32, 0.9, 1.8) * math.sqrt(FRONT)
    position = jnp.arange(FRONT)
    identity = position[:, None] == position[None, :]
    return symmetric + jnp.where(identity[None, :, :], diagonal[:, :, None], 0.0)


def draw_child_map(key, part):
    key = jax.random.fold_in(key, 2)
    schur_tiles = FRONT // TILE - PANEL // TILE
    parity = jax.random.randint(key, (FRONTS, schur_tiles), 0, 2, jnp.int32)
    position = jnp.arange(schur_tiles, dtype=jnp.int32)
    parity = jnp.where(position[None, :] == 0, 0, jnp.where(position[None, :] == schur_tiles - 1, 1, parity))
    return (2 * (position[None, :] + PANEL // TILE) + parity).astype(jnp.int32)


def level_of(own_key, extent, pieces, smallest, top_value):
    def one(axis_at, parts):
        steps = jax.random.uniform(jax.random.fold_in(jax.random.fold_in(own_key, 6), axis_at), (parts,), jnp.float32, smallest / len(pieces), top_value / len(pieces))
        return jnp.repeat(jnp.exp(steps), extent[axis_at] // parts).reshape((-1,) + (1,) * (len(extent) - axis_at - 1))

    loudness = one(*pieces[0])
    for cut in pieces[1:]:
        loudness = loudness * one(*cut)
    return loudness


def centred(key, dims, width, limit, pieces=(), kind=jnp.bfloat16):
    values = width * jax.random.normal(key, dims, jnp.float32)
    if pieces:
        values = values * level_of(key, dims, pieces, -0.22, 0.18)
    return jnp.clip(values, -limit, limit).astype(kind)


def setup_inputs(seed: int = 0) -> dict:
    seeds = jax.random.split(jax.random.key(seed), 4)
    return {
        "front_block": draw_front_block(jax.random.fold_in(seeds[3], 71), 0),
        "child_map": draw_child_map(jax.random.fold_in(seeds[3], 71), 0),
        "parent_entries": centred(seeds[2], (PARENT, PARENT), 0.25, 2.0, ((0, 32), (1, 8)), jnp.float32),
    }


def spread(block, row_bits, col_bits):
    row_count = row_bits.shape[0]
    col_count = col_bits.shape[0]
    halves = jnp.arange(2, dtype=jnp.int32)
    row_tiles = block.reshape(row_count, 1, TILE, col_count * TILE)
    doubled = jnp.where(row_bits.reshape(row_count, 1, 1, 1) == halves.reshape(1, 2, 1, 1), row_tiles, 0.0)
    doubled = doubled.reshape(2 * row_count * TILE, col_count, 1, TILE)
    widened = jnp.where(col_bits.reshape(1, col_count, 1, 1) == halves.reshape(1, 1, 2, 1), doubled, 0.0)
    return widened.reshape(2 * row_count * TILE, 2 * col_count * TILE)

def reference(front_block, child_map, parent_entries):
    tile_total = FRONT // TILE
    pivot_tiles = PANEL // TILE
    parent = parent_entries
    for sibling in range(child_map.shape[0]):
        matrix = front_block[sibling]
        pivot_factor = jnp.linalg.cholesky(matrix[:PANEL, :PANEL])
        lower_panel = jax.scipy.linalg.solve_triangular(pivot_factor, matrix[:, :PANEL].T, lower=True).T
        upper_panel = jax.scipy.linalg.solve_triangular(pivot_factor, matrix[:PANEL, :], lower=True)
        schur_block = matrix - jnp.dot(lower_panel.astype(jnp.float32), upper_panel.astype(jnp.float32), precision=lax.Precision.HIGHEST, preferred_element_type=jnp.float32)
        tile_bits = jnp.concatenate([-jnp.ones((pivot_tiles,), jnp.int32), child_map[sibling] - 2 * (jnp.arange(tile_total - pivot_tiles, dtype=jnp.int32) + pivot_tiles)])
        parent = parent + spread(schur_block, tile_bits, tile_bits)
    return parent
```

```python
import functools

import jax
import jax.numpy as jnp
from jax import lax
from jax.experimental import pallas as pl
from jax.experimental.pallas import tpu as pltpu
from jax.sharding import PartitionSpec as P

PANEL = 512
TILE = 128
FRONT_AXES = ("front", "row")
PLANE_AXES = ("row", "col")
PIECES = 4
PIECE = 256
HIGHEST = lax.Precision.HIGHEST
HIGH = lax.Precision.HIGH


def eliminate(block):
    groups = TILE // 8
    tiles = [block[8 * i : 8 * i + 8, :] for i in range(groups)]
    lane = lax.broadcasted_iota(jnp.int32, (8, TILE), 1)
    sublane = lax.broadcasted_iota(jnp.int32, (8, TILE), 0)
    for j in range(TILE):
        t, s = j // 8, j % 8
        row = tiles[t][s : s + 1, :]
        inverse = 1.0 / jnp.broadcast_to(row[:, j : j + 1], (8, TILE))
        here = lane == j
        for i in range(t, groups):
            factor = jnp.broadcast_to(tiles[i][:, j : j + 1], (8, TILE)) * inverse
            new = jnp.where(here, -factor, tiles[i] - factor * row)
            tiles[i] = jnp.where(sublane > s, new, tiles[i]) if i == t else new
    out = []
    for i in range(groups):
        at = sublane + 8 * i
        pivot = jnp.sum(jnp.where(lane == at, tiles[i], 0.0), axis=1, keepdims=True)
        unit = jnp.where(lane < at, tiles[i], jnp.where(lane == at, 1.0, 0.0))
        out.append(unit * lax.rsqrt(pivot))
    return jnp.concatenate(out, axis=0)


def factor_kernel(pivot_ref, out_ref, work):
    rows = lax.broadcasted_iota(jnp.int32, (PANEL, PANEL), 0)
    columns = lax.broadcasted_iota(jnp.int32, (PANEL, PANEL), 1)
    work[:, :PANEL] = pivot_ref[...]
    work[:, PANEL:] = jnp.where(rows == columns, 1.0, 0.0)

    def step(k, carry):
        start = pl.multiple_of(k * TILE, TILE)
        inverse = eliminate(work[pl.ds(start, TILE), pl.ds(start, TILE)])
        solved = jnp.dot(
            inverse,
            work[pl.ds(start, TILE), :],
            precision=HIGHEST,
            preferred_element_type=jnp.float32,
        )
        left = solved[:, :PANEL]
        column = lax.broadcasted_iota(jnp.int32, left.shape, 1)
        left = jnp.where(column >= start + TILE, left, 0.0)
        work[...] -= lax.dot_general(
            left,
            solved,
            (((0,), (0,)), ((), ())),
            precision=HIGHEST,
            preferred_element_type=jnp.float32,
        )
        work[pl.ds(start, TILE), :] = solved
        return carry

    lax.fori_loop(0, PANEL // TILE, step, 0)
    out_ref[...] = work[:, PANEL:]


def inverse_factor(pivot_block):
    return pl.pallas_call(
        factor_kernel,
        out_shape=jax.ShapeDtypeStruct((PANEL, PANEL), jnp.float32),
        in_specs=[pl.BlockSpec(memory_space=pltpu.VMEM)],
        out_specs=pl.BlockSpec(memory_space=pltpu.VMEM),
        scratch_shapes=[pltpu.VMEM((PANEL, 2 * PANEL), jnp.float32)],
        compiler_params=pltpu.CompilerParams(vmem_limit_bytes=24 * 2**20),
        cost_estimate=pl.CostEstimate(
            flops=10_000_000_000, bytes_accessed=2 * 2**20, transcendentals=0
        ),
        name="inverse_factor",
    )(pivot_block)


def extend_add_kernel(place_ref, map_ref, parent_ref, *refs):
    pieces, out_ref = refs[:PIECES], refs[PIECES]
    my_front, my_row, my_col = place_ref[0], place_ref[1], place_ref[2]
    local_row, group = pl.program_id(0), pl.program_id(1)
    col_tiles = pieces[0].shape[1] // TILE
    pivot_tiles = PANEL // TILE

    def bit(front, tile):
        found = map_ref[front, jnp.maximum(tile - pivot_tiles, 0)] - 2 * tile
        return jnp.where(tile >= pivot_tiles, found, -1)

    row_tile = 2 * (8 * my_front + my_row) + local_row
    fronts = [my_front ^ (my_row & 3) ^ k for k in range(PIECES)]
    row_bits = [bit(front, row_tile) for front in fronts]
    for u in range(col_tiles):
        col_tile = 8 * my_col + group * col_tiles + u
        col_bits = [bit(front, col_tile) for front in fronts]
        blocks = [piece[:, u * TILE : (u + 1) * TILE] for piece in pieces]
        for a in range(2):
            for b in range(2):
                rows = slice(a * TILE, (a + 1) * TILE)
                columns = slice((2 * u + b) * TILE, (2 * u + b + 1) * TILE)
                total = parent_ref[rows, columns]
                for k in range(PIECES):
                    hit = jnp.logical_and(row_bits[k] == a, col_bits[k] == b)
                    total += jnp.where(hit, blocks[k], 0.0)
                out_ref[rows, columns] = total


def extend_add(place, child_map, parent, pieces):
    groups = 2
    rows, columns = pieces[0].shape
    wide = columns // groups
    piece_spec = pl.BlockSpec((TILE, wide), lambda i, g, *_: (i, g))
    parent_spec = pl.BlockSpec((2 * TILE, 2 * wide), lambda i, g, *_: (i, g))
    return pl.pallas_call(
        extend_add_kernel,
        out_shape=jax.ShapeDtypeStruct(parent.shape, jnp.float32),
        grid_spec=pltpu.PrefetchScalarGridSpec(
            num_scalar_prefetch=2,
            grid=(rows // TILE, groups),
            in_specs=[parent_spec] + [piece_spec] * PIECES,
            out_specs=parent_spec,
        ),
        cost_estimate=pl.CostEstimate(
            flops=8 * 2**20, bytes_accessed=12 * 2**20, transcendentals=0
        ),
        name="extend_add",
    )(place, child_map, parent, *pieces)


def fan_out(parts, axis, numbers):
    received = [lax.ppermute(parts[k], axis, [numbers(k)]) for k in range(1, 8)]
    return functools.reduce(jnp.add, received)


def local(front_block, child_map, parent_entries):
    matrix = front_block[0]
    my_front = lax.axis_index("front")
    my_row = lax.axis_index("row")
    my_col = lax.axis_index("col")
    quarter = my_row & 3
    chunk = PANEL // 8

    with jax.named_scope("pivot_spread"):
        parts = [matrix[chunk * k : chunk * (k + 1), :PANEL] for k in range(8)]
        part = fan_out(parts, PLANE_AXES, lambda k: (0, k))
        part = jnp.where(my_col == 0, parts[0], part)
        far = fan_out([part] * 8, "row", lambda k: (0, k))
        part = jnp.where(my_row == 0, part, far)
        pivot_block = lax.all_gather(part, "col", tiled=True)

    with jax.named_scope("panel_spread"):
        parts = [matrix[chunk * k : chunk * (k + 1), :] for k in range(8)]
        part = fan_out(parts, "row", lambda k: (0, k))
        part = jnp.where(my_row == 0, parts[0], part)
        panel_top = lax.all_gather(part, "row", tiled=True)

    with jax.named_scope("row_panel"):
        half = my_col & 1
        start = PIECE * quarter
        mine = lax.dynamic_slice_in_dim(panel_top, start + TILE * half, TILE, 1)
        other = lax.dynamic_slice_in_dim(panel_top, start + TILE * (1 - half), TILE, 1)
        pairs = [
            (r * 8 + 2 * y + r // 4, r * 8 + 2 * y + 1 - r // 4) for r in range(8) for y in range(4)
        ]
        other = lax.ppermute(other, PLANE_AXES, pairs)
        mine = jnp.where(half == my_row // 4, mine, other)
        row_panel = lax.all_gather(mine, "col")

    with jax.named_scope("rows_along_z"):
        arrived = []
        for k in range(PIECES):
            piece = (my_row // 2) ^ k ^ my_front
            sent = lax.dynamic_slice_in_dim(matrix, piece * PIECE, PIECE, 0)
            pairs = [
                (f * 8 + r, f * 8 + 4 * (r % 2) + ((r // 2) ^ k ^ f))
                for f in range(4)
                for r in range(8)
            ]
            arrived.append(lax.ppermute(sent, FRONT_AXES, pairs))

    with jax.named_scope("factor"):
        inverse = inverse_factor(pivot_block)
    with jax.named_scope("solve"):
        upper = jnp.dot(inverse, panel_top, precision=HIGH, preferred_element_type=jnp.float32)
        lower = lax.dot_general(
            row_panel,
            inverse,
            (((1,), (1,)), ((), ())),
            precision=HIGH,
            preferred_element_type=jnp.float32,
        ).reshape(PIECES * PIECE, PANEL)

    pieces = []
    for k in range(PIECES):
        with jax.named_scope("schur"):
            target = quarter ^ k ^ my_front
            left = lax.dynamic_slice_in_dim(lower, target * PIECE, PIECE, 0)
            schur = arrived[k] - jnp.dot(
                left, upper, precision=HIGH, preferred_element_type=jnp.float32
            )
        with jax.named_scope("to_parent"):
            pairs = [(f * 8 + r, (f ^ (r & 3) ^ k) * 8 + r) for f in range(4) for r in range(8)]
            pieces.append(lax.ppermute(schur, FRONT_AXES, pairs))

    with jax.named_scope("extend_add"):
        place = jnp.stack([my_front, my_row, my_col]).astype(jnp.int32)
        return extend_add(place, child_map, parent_entries, pieces)


def solution(mesh):
    in_specs = (P("front", "row", "col"), P(), P(("front", "row"), "col"))
    out_specs = P(("front", "row"), "col")
    return jax.shard_map(local, mesh=mesh, in_specs=in_specs, out_specs=out_specs, check_vma=False)
```

```python
import functools

import jax
import jax.numpy as jnp
from jax import lax
from jax.experimental import pallas as pl
from jax.experimental.pallas import tpu as pltpu
from jax.sharding import PartitionSpec as P

PANEL = 512
TILE = 128
FRONT_AXES = ("front", "row")
PLANE_AXES = ("row", "col")
PIECES = 4
PIECE = 256
HIGHEST = lax.Precision.HIGHEST
HIGH = lax.Precision.HIGH


def eliminate(block):
    groups = TILE // 8
    tiles = [block[8 * i : 8 * i + 8, :] for i in range(groups)]
    sublane = lax.broadcasted_iota(jnp.int32, (8, TILE), 0)
    lanes = lax.broadcasted_iota(jnp.int32, (8, TILE), 1)
    lane = lax.broadcasted_iota(jnp.int32, (1, TILE), 1)
    out = []
    for t in range(groups):
        j = 8 * t
        columns = [
            [jnp.broadcast_to(tiles[i][:, j + k : j + k + 1], (8, TILE)) for k in range(8)]
            for i in range(t, groups)
        ]
        pivots = [[columns[0][k][m : m + 1, :] for k in range(8)] for m in range(8)]
        rows, inverses = [], []
        final = None
        for k in range(8):
            factors = [pivots[m][k] * inverses[m] for m in range(k)]
            for c in range(k, 8):
                for m in range(k):
                    pivots[k][c] -= factors[m] * pivots[m][c]
            inverses.append(1.0 / pivots[k][k])
            unit = jnp.where(lane == j + k, 1.0, 0.0)
            row = jnp.where((lane >= j) & (lane < j + 8), unit, tiles[t][k : k + 1, :])
            for m in range(k):
                row -= factors[m] * rows[m]
            rows.append(row)
            scaled = jnp.where(lane <= j + k, row, 0.0) * lax.rsqrt(pivots[k][k])
            scaled = jnp.broadcast_to(scaled, (8, TILE))
            final = scaled if k == 0 else jnp.where(sublane == k, scaled, final)
        out.append(final)
        for i in range(t + 1, groups):
            factors = []
            new = jnp.where((lanes >= j) & (lanes < j + 8), 0.0, tiles[i])
            for k in range(8):
                value = columns[i - t][k]
                for m in range(k):
                    value -= factors[m] * pivots[m][k]
                factors.append(value * inverses[k])
                new -= factors[k] * rows[k]
            tiles[i] = new
    return jnp.concatenate(out, axis=0)


def exact_dot(left, right, contract):
    return lax.dot_general(
        left,
        right,
        (contract, ((), ())),
        precision=HIGHEST,
        preferred_element_type=jnp.float32,
    )


def factor_kernel(place_ref, *refs):
    parts, out_ref, work = refs[:8], refs[8], refs[9]
    my_col = place_ref[2]
    chunk = PANEL // 8
    for j in range(8):
        start = pl.multiple_of(chunk * (my_col ^ j), chunk)
        work[pl.ds(start, chunk), :] = parts[j][...]
    for k in range(PANEL // TILE):
        low, high = k * TILE, (k + 1) * TILE
        inverse = eliminate(work[low:high, low:high])
        work[low:high, low:high] = inverse
        if k > 0:
            work[low:high, :low] = exact_dot(inverse, work[low:high, :low], ((1,), (0,)))
        if high < PANEL:
            right = exact_dot(inverse, work[low:high, high:], ((1,), (0,)))
            work[low:high, high:] = right
            work[high:, low:high] = jnp.zeros((PANEL - high, TILE), jnp.float32)
            work[high:, :] -= exact_dot(right, work[low:high, :], ((0,), (0,)))
            work[low:high, high:] = jnp.zeros_like(right)
    out_ref[...] = work[...]


def inverse_factor(place, parts):
    return pl.pallas_call(
        factor_kernel,
        out_shape=jax.ShapeDtypeStruct((PANEL, PANEL), jnp.float32),
        in_specs=[pl.BlockSpec(memory_space=pltpu.SMEM)]
        + [pl.BlockSpec(memory_space=pltpu.VMEM)] * 8,
        out_specs=pl.BlockSpec(memory_space=pltpu.VMEM),
        scratch_shapes=[pltpu.VMEM((PANEL, PANEL), jnp.float32)],
        compiler_params=pltpu.CompilerParams(vmem_limit_bytes=24 * 2**20),
        cost_estimate=pl.CostEstimate(
            flops=10_000_000_000, bytes_accessed=2 * 2**20, transcendentals=0
        ),
        name="inverse_factor",
    )(place, *parts)


def split(value):
    high = value.astype(jnp.bfloat16)
    return high, (value - high.astype(jnp.float32)).astype(jnp.bfloat16)


def split_dot(left, right, contract):
    def dot(a, b):
        return lax.dot_general(a, b, (contract, ((), ())), preferred_element_type=jnp.float32)

    return dot(left[0], right[0]) + (dot(left[0], right[1]) + dot(left[1], right[0]))


def solve_kernel(inverse_ref, top_ref, rows_ref, lower_ref, upper_ref):
    inverse = split(inverse_ref[...])
    for j in range(8):
        lower_ref[TILE * j : TILE * (j + 1), :] = split_dot(
            split(rows_ref[j]), inverse, ((0,), (1,))
        )
    wide = 256
    for j in range(0, top_ref.shape[1], wide):
        upper_ref[:, j : j + wide] = split_dot(
            inverse, split(top_ref[:, j : j + wide]), ((1,), (0,))
        )


def solve(inverse, panel_top, row_panel):
    vmem = pl.BlockSpec(memory_space=pltpu.VMEM)
    return pl.pallas_call(
        solve_kernel,
        out_shape=(
            jax.ShapeDtypeStruct((PIECES * PIECE, PANEL), jnp.float32),
            jax.ShapeDtypeStruct(panel_top.shape, jnp.float32),
        ),
        in_specs=[vmem] * 3,
        out_specs=(vmem, vmem),
        compiler_params=pltpu.CompilerParams(vmem_limit_bytes=40 * 2**20),
        cost_estimate=pl.CostEstimate(
            flops=6_000_000_000, bytes_accessed=9 * 2**20, transcendentals=0
        ),
        name="solve",
    )(inverse, panel_top, row_panel)


def extend_add_kernel(place_ref, map_ref, parent_ref, *refs):
    pieces, out_ref = refs[:PIECES], refs[PIECES]
    my_front, my_row, my_col = place_ref[0], place_ref[1], place_ref[2]
    local_row, group = pl.program_id(0), pl.program_id(1)
    col_tiles = pieces[0].shape[1] // TILE
    pivot_tiles = PANEL // TILE

    def bit(front, tile):
        found = map_ref[front, jnp.maximum(tile - pivot_tiles, 0)] - 2 * tile
        return jnp.where(tile >= pivot_tiles, found, -1)

    row_tile = 2 * (8 * my_front + my_row) + local_row
    fronts = [my_front ^ (my_row & 3) ^ k for k in range(PIECES)]
    row_bits = [bit(front, row_tile) for front in fronts]
    for u in range(col_tiles):
        col_tile = 8 * my_col + group * col_tiles + u
        col_bits = [bit(front, col_tile) for front in fronts]
        blocks = [piece[:, u * TILE : (u + 1) * TILE] for piece in pieces]
        for a in range(2):
            for b in range(2):
                rows = slice(a * TILE, (a + 1) * TILE)
                columns = slice((2 * u + b) * TILE, (2 * u + b + 1) * TILE)
                total = parent_ref[rows, columns]
                for k in range(PIECES):
                    hit = jnp.logical_and(row_bits[k] == a, col_bits[k] == b)
                    total += jnp.where(hit, blocks[k], 0.0)
                out_ref[rows, columns] = total


def extend_add(place, child_map, parent, pieces):
    groups = 2
    rows, columns = pieces[0].shape
    wide = columns // groups
    piece_spec = pl.BlockSpec((TILE, wide), lambda i, g, *_: (i, g))
    parent_spec = pl.BlockSpec((2 * TILE, 2 * wide), lambda i, g, *_: (i, g))
    return pl.pallas_call(
        extend_add_kernel,
        out_shape=jax.ShapeDtypeStruct(parent.shape, jnp.float32),
        grid_spec=pltpu.PrefetchScalarGridSpec(
            num_scalar_prefetch=2,
            grid=(rows // TILE, groups),
            in_specs=[parent_spec] + [piece_spec] * PIECES,
            out_specs=parent_spec,
        ),
        cost_estimate=pl.CostEstimate(
            flops=8 * 2**20, bytes_accessed=12 * 2**20, transcendentals=0
        ),
        name="extend_add",
    )(place, child_map, parent, *pieces)


def fan_out(parts, axis, numbers):
    received = [lax.ppermute(parts[k], axis, [numbers(k)]) for k in range(1, 8)]
    return functools.reduce(jnp.add, received)


def local(front_block, child_map, parent_entries):
    matrix = front_block[0]
    my_front = lax.axis_index("front")
    my_row = lax.axis_index("row")
    my_col = lax.axis_index("col")
    quarter = my_row & 3
    chunk = PANEL // 8

    place = jnp.stack([my_front, my_row, my_col]).astype(jnp.int32)

    with jax.named_scope("pivot_to_columns"):
        parts = [matrix[chunk * k : chunk * (k + 1), :PANEL] for k in range(8)]
        part = fan_out(parts, PLANE_AXES, lambda k: (0, k))
        part = jnp.where(my_col == 0, parts[0], part)

    with jax.named_scope("panel_scatter"):
        parts = [matrix[chunk * k : chunk * (k + 1), :] for k in range(8)]
        panel_part = fan_out(parts, "row", lambda k: (0, k))
        panel_part = jnp.where(my_row == 0, parts[0], panel_part)
        part, panel_part = lax.optimization_barrier((part, panel_part))

    with jax.named_scope("pivot_along_z"):
        for distance in (4, 2, 1):
            pairs = [(r, r + distance) for r in range(0, 8, 2 * distance)]
            far = lax.ppermute(part, "row", pairs)
            part = jnp.where((my_row & (2 * distance - 1)) == distance, far, part)

    with jax.named_scope("pivot_in_plane"):
        parts = [part] + [
            lax.ppermute(part, "col", [(c, c ^ j) for c in range(8)]) for j in range(1, 8)
        ]

    with jax.named_scope("panel_gather"):
        panel_top = lax.all_gather(panel_part, "row", tiled=True)

    with jax.named_scope("rows_along_z"):
        panel_top, matrix = lax.optimization_barrier((panel_top, matrix))
        arrived = []
        for k in range(PIECES):
            piece = (my_row // 2) ^ k ^ my_front
            sent = lax.dynamic_slice_in_dim(matrix, piece * PIECE, PIECE, 0)
            pairs = [
                (f * 8 + r, f * 8 + 4 * (r % 2) + ((r // 2) ^ k ^ f))
                for f in range(4)
                for r in range(8)
            ]
            arrived.append(lax.ppermute(sent, FRONT_AXES, pairs))

    with jax.named_scope("row_panel"):
        panel_top, *parts = lax.optimization_barrier((panel_top, *parts))
        half = my_col & 1
        start = PIECE * quarter
        mine = lax.dynamic_slice_in_dim(panel_top, start + TILE * half, TILE, 1)
        other = lax.dynamic_slice_in_dim(panel_top, start + TILE * (1 - half), TILE, 1)
        pairs = [
            (r * 8 + 2 * y + r // 4, r * 8 + 2 * y + 1 - r // 4) for r in range(8) for y in range(4)
        ]
        other = lax.ppermute(other, PLANE_AXES, pairs)
        mine = jnp.where(half == my_row // 4, mine, other)
        row_panel = lax.all_gather(mine, "col")

    with jax.named_scope("factor"):
        inverse = inverse_factor(place, parts)

    with jax.named_scope("solve"):
        lower, upper = solve(inverse, panel_top, row_panel)

    pieces = []
    for k in range(PIECES):
        with jax.named_scope("schur"):
            target = quarter ^ k ^ my_front
            left = lax.dynamic_slice_in_dim(lower, target * PIECE, PIECE, 0)
            schur = arrived[k] - jnp.dot(
                left, upper, precision=HIGH, preferred_element_type=jnp.float32
            )
        with jax.named_scope("to_parent"):
            pairs = [(f * 8 + r, (f ^ (r & 3) ^ k) * 8 + r) for f in range(4) for r in range(8)]
            pieces.append(lax.ppermute(schur, FRONT_AXES, pairs))

    with jax.named_scope("extend_add"):
        return extend_add(place, child_map, parent_entries, pieces)


def solution(mesh):
    in_specs = (P("front", "row", "col"), P(), P(("front", "row"), "col"))
    out_specs = P(("front", "row"), "col")
    return jax.shard_map(local, mesh=mesh, in_specs=in_specs, out_specs=out_specs, check_vma=False)
```

```python
import functools

import jax
import jax.numpy as jnp
from jax import lax
from jax.experimental import pallas as pl
from jax.experimental.pallas import tpu as pltpu
from jax.sharding import PartitionSpec as P

PANEL = 512
TILE = 128
FRONT_AXES = ("front", "row")
PLANE_AXES = ("row", "col")
PIECES = 4
PIECE = 256
HIGHEST = lax.Precision.HIGHEST
HIGH = lax.Precision.HIGH


def eliminate(block):
    groups = TILE // 8
    tiles = [block[8 * i : 8 * i + 8, :] for i in range(groups)]
    sublane = lax.broadcasted_iota(jnp.int32, (8, TILE), 0)
    lanes = lax.broadcasted_iota(jnp.int32, (8, TILE), 1)
    lane = lax.broadcasted_iota(jnp.int32, (1, TILE), 1)
    out = []
    for t in range(groups):
        j = 8 * t
        columns = [
            [jnp.broadcast_to(tiles[i][:, j + k : j + k + 1], (8, TILE)) for k in range(8)]
            for i in range(t, groups)
        ]
        pivots = [[columns[0][k][m : m + 1, :] for k in range(8)] for m in range(8)]
        rows, inverses = [], []
        final = None
        for k in range(8):
            factors = [pivots[m][k] * inverses[m] for m in range(k)]
            for c in range(k, 8):
                for m in range(k):
                    pivots[k][c] -= factors[m] * pivots[m][c]
            inverses.append(1.0 / pivots[k][k])
            unit = jnp.where(lane == j + k, 1.0, 0.0)
            row = jnp.where((lane >= j) & (lane < j + 8), unit, tiles[t][k : k + 1, :])
            for m in range(k):
                row -= factors[m] * rows[m]
            rows.append(row)
            scaled = jnp.where(lane <= j + k, row, 0.0) * lax.rsqrt(pivots[k][k])
            scaled = jnp.broadcast_to(scaled, (8, TILE))
            final = scaled if k == 0 else jnp.where(sublane == k, scaled, final)
        out.append(final)
        for i in range(t + 1, groups):
            factors = []
            new = jnp.where((lanes >= j) & (lanes < j + 8), 0.0, tiles[i])
            for k in range(8):
                value = columns[i - t][k]
                for m in range(k):
                    value -= factors[m] * pivots[m][k]
                factors.append(value * inverses[k])
                new -= factors[k] * rows[k]
            tiles[i] = new
    return jnp.concatenate(out, axis=0)


def exact_dot(left, right, contract):
    return lax.dot_general(
        left,
        right,
        (contract, ((), ())),
        precision=HIGHEST,
        preferred_element_type=jnp.float32,
    )


def factor_kernel(pivot_ref, out_ref, work):
    work[...] = pivot_ref[...]
    for k in range(PANEL // TILE):
        low, high = k * TILE, (k + 1) * TILE
        inverse = eliminate(work[low:high, low:high])
        work[low:high, low:high] = inverse
        if k > 0:
            work[low:high, :low] = exact_dot(inverse, work[low:high, :low], ((1,), (0,)))
        if high < PANEL:
            right = exact_dot(inverse, work[low:high, high:], ((1,), (0,)))
            work[low:high, high:] = right
            work[high:, low:high] = jnp.zeros((PANEL - high, TILE), jnp.float32)
            work[high:, :] -= exact_dot(right, work[low:high, :], ((0,), (0,)))
            work[low:high, high:] = jnp.zeros_like(right)
    out_ref[...] = work[...]


def inverse_factor(pivot_block):
    return pl.pallas_call(
        factor_kernel,
        out_shape=jax.ShapeDtypeStruct((PANEL, PANEL), jnp.float32),
        in_specs=[pl.BlockSpec(memory_space=pltpu.VMEM)],
        out_specs=pl.BlockSpec(memory_space=pltpu.VMEM),
        scratch_shapes=[pltpu.VMEM((PANEL, PANEL), jnp.float32)],
        compiler_params=pltpu.CompilerParams(vmem_limit_bytes=24 * 2**20),
        cost_estimate=pl.CostEstimate(
            flops=300_000_000, bytes_accessed=2 * 2**20, transcendentals=0
        ),
        name="inverse_factor",
    )(pivot_block)


def split(value):
    high = value.astype(jnp.bfloat16)
    return high, (value - high.astype(jnp.float32)).astype(jnp.bfloat16)


def split_dot(left, right, contract):
    def dot(a, b):
        return lax.dot_general(a, b, (contract, ((), ())), preferred_element_type=jnp.float32)

    return dot(left[0], right[0]) + (dot(left[0], right[1]) + dot(left[1], right[0]))


def solve_kernel(inverse_ref, top_ref, rows_ref, lower_ref, upper_ref):
    inverse = split(inverse_ref[...])
    for j in range(8):
        lower_ref[TILE * j : TILE * (j + 1), :] = split_dot(
            split(rows_ref[j]), inverse, ((0,), (1,))
        )
    wide = 256
    for j in range(0, top_ref.shape[1], wide):
        upper_ref[:, j : j + wide] = split_dot(
            inverse, split(top_ref[:, j : j + wide]), ((1,), (0,))
        )


def solve(inverse, panel_top, row_panel):
    vmem = pl.BlockSpec(memory_space=pltpu.VMEM)
    return pl.pallas_call(
        solve_kernel,
        out_shape=(
            jax.ShapeDtypeStruct((PIECES * PIECE, PANEL), jnp.float32),
            jax.ShapeDtypeStruct(panel_top.shape, jnp.float32),
        ),
        in_specs=[vmem] * 3,
        out_specs=(vmem, vmem),
        compiler_params=pltpu.CompilerParams(vmem_limit_bytes=40 * 2**20),
        cost_estimate=pl.CostEstimate(
            flops=3_000_000_000, bytes_accessed=9 * 2**20, transcendentals=0
        ),
        name="solve",
    )(inverse, panel_top, row_panel)


def extend_add_kernel(place_ref, map_ref, parent_ref, *refs):
    pieces, out_ref = refs[:PIECES], refs[PIECES]
    my_front, my_row, my_col = place_ref[0], place_ref[1], place_ref[2]
    local_row, group = pl.program_id(0), pl.program_id(1)
    col_tiles = pieces[0].shape[1] // TILE
    pivot_tiles = PANEL // TILE

    def bit(front, tile):
        found = map_ref[front, jnp.maximum(tile - pivot_tiles, 0)] - 2 * tile
        return jnp.where(tile >= pivot_tiles, found, -1)

    row_tile = 2 * (8 * my_front + my_row) + local_row
    fronts = [my_front ^ (my_row & 3) ^ k for k in range(PIECES)]
    row_bits = [bit(front, row_tile) for front in fronts]
    for u in range(col_tiles):
        col_tile = 8 * my_col + group * col_tiles + u
        col_bits = [bit(front, col_tile) for front in fronts]
        blocks = [piece[:, u * TILE : (u + 1) * TILE] for piece in pieces]
        for a in range(2):
            for b in range(2):
                rows = slice(a * TILE, (a + 1) * TILE)
                columns = slice((2 * u + b) * TILE, (2 * u + b + 1) * TILE)
                total = parent_ref[rows, columns]
                for k in range(PIECES):
                    hit = jnp.logical_and(row_bits[k] == a, col_bits[k] == b)
                    total += jnp.where(hit, blocks[k], 0.0)
                out_ref[rows, columns] = total


def extend_add(place, child_map, parent, pieces):
    groups = 2
    rows, columns = pieces[0].shape
    wide = columns // groups
    piece_spec = pl.BlockSpec((TILE, wide), lambda i, g, *_: (i, g))
    parent_spec = pl.BlockSpec((2 * TILE, 2 * wide), lambda i, g, *_: (i, g))
    return pl.pallas_call(
        extend_add_kernel,
        out_shape=jax.ShapeDtypeStruct(parent.shape, jnp.float32),
        grid_spec=pltpu.PrefetchScalarGridSpec(
            num_scalar_prefetch=2,
            grid=(rows // TILE, groups),
            in_specs=[parent_spec] + [piece_spec] * PIECES,
            out_specs=parent_spec,
        ),
        cost_estimate=pl.CostEstimate(
            flops=8 * 2**20, bytes_accessed=12 * 2**20, transcendentals=0
        ),
        name="extend_add",
    )(place, child_map, parent, *pieces)


def fan_out(parts, axis, numbers):
    received = [lax.ppermute(parts[k], axis, [numbers(k)]) for k in range(1, 8)]
    return functools.reduce(jnp.add, received)


def local(front_block, child_map, parent_entries):
    matrix = front_block[0]
    my_front = lax.axis_index("front")
    my_row = lax.axis_index("row")
    my_col = lax.axis_index("col")
    quarter = my_row & 3
    chunk = PANEL // 8

    place = jnp.stack([my_front, my_row, my_col]).astype(jnp.int32)

    with jax.named_scope("pivot_to_columns"):
        parts = [matrix[chunk * k : chunk * (k + 1), :PANEL] for k in range(8)]
        part = fan_out(parts, PLANE_AXES, lambda k: (0, k))
        part = jnp.where(my_col == 0, parts[0], part)

    with jax.named_scope("panel_scatter"):
        parts = [matrix[chunk * k : chunk * (k + 1), :] for k in range(8)]
        panel_part = fan_out(parts, "row", lambda k: (0, k))
        panel_part = jnp.where(my_row == 0, parts[0], panel_part)

    with jax.named_scope("pivot_along_z"):
        for distance in (4, 2, 1):
            pairs = [(r, r + distance) for r in range(0, 8, 2 * distance)]
            far = lax.ppermute(part, "row", pairs)
            part = jnp.where((my_row & (2 * distance - 1)) == distance, far, part)

    with jax.named_scope("pivot_in_plane"):
        pivot_block = lax.all_gather(part, "col", tiled=True)

    with jax.named_scope("panel_gather"):
        panel_top = lax.all_gather(panel_part, "row", tiled=True)

    with jax.named_scope("rows_along_z"):
        panel_top, matrix = lax.optimization_barrier((panel_top, matrix))
        arrived = []
        for k in range(PIECES):
            piece = (my_row // 2) ^ k ^ my_front
            sent = lax.dynamic_slice_in_dim(matrix, piece * PIECE, PIECE, 0)
            pairs = [
                (f * 8 + r, f * 8 + 4 * (r % 2) + ((r // 2) ^ k ^ f))
                for f in range(4)
                for r in range(8)
            ]
            arrived.append(lax.ppermute(sent, FRONT_AXES, pairs))

    with jax.named_scope("row_panel"):
        half = my_col & 1
        start = PIECE * quarter
        mine = lax.dynamic_slice_in_dim(panel_top, start + TILE * half, TILE, 1)
        other = lax.dynamic_slice_in_dim(panel_top, start + TILE * (1 - half), TILE, 1)
        pairs = [
            (r * 8 + 2 * y + r // 4, r * 8 + 2 * y + 1 - r // 4) for r in range(8) for y in range(4)
        ]
        other = lax.ppermute(other, PLANE_AXES, pairs)
        mine = jnp.where(half == my_row // 4, mine, other)
        row_panel = lax.all_gather(mine, "col")

    with jax.named_scope("factor"):
        inverse = inverse_factor(pivot_block)

    with jax.named_scope("solve"):
        lower, upper = solve(inverse, panel_top, row_panel)

    pieces = []
    for k in range(PIECES):
        with jax.named_scope("schur"):
            target = quarter ^ k ^ my_front
            left = lax.dynamic_slice_in_dim(lower, target * PIECE, PIECE, 0)
            schur = arrived[k] - jnp.dot(
                left, upper, precision=HIGH, preferred_element_type=jnp.float32
            )
        with jax.named_scope("to_parent"):
            pairs = [(f * 8 + r, (f ^ (r & 3) ^ k) * 8 + r) for f in range(4) for r in range(8)]
            pieces.append(lax.ppermute(schur, FRONT_AXES, pairs))

    with jax.named_scope("extend_add"):
        return extend_add(place, child_map, parent_entries, pieces)


def solution(mesh):
    in_specs = (P("front", "row", "col"), P(), P(("front", "row"), "col"))
    out_specs = P(("front", "row"), "col")
    return jax.shard_map(local, mesh=mesh, in_specs=in_specs, out_specs=out_specs, check_vma=False)
```

```python
import functools

import jax
import jax.numpy as jnp
from jax import lax
from jax.experimental import pallas as pl
from jax.experimental.pallas import tpu as pltpu
from jax.sharding import PartitionSpec as P

PANEL = 512
TILE = 128
FRONT_AXES = ("front", "row")
PLANE_AXES = ("row", "col")
PIECES = 4
PIECE = 256
HIGHEST = lax.Precision.HIGHEST
HIGH = lax.Precision.HIGH


def eliminate(block):
    groups = TILE // 8
    tiles = [block[8 * i : 8 * i + 8, :] for i in range(groups)]
    sublane = lax.broadcasted_iota(jnp.int32, (8, TILE), 0)
    lanes = lax.broadcasted_iota(jnp.int32, (8, TILE), 1)
    lane = lax.broadcasted_iota(jnp.int32, (1, TILE), 1)
    out = []
    for t in range(groups):
        j = 8 * t
        columns = [
            [jnp.broadcast_to(tiles[i][:, j + k : j + k + 1], (8, TILE)) for k in range(8)]
            for i in range(t, groups)
        ]
        pivots = [[columns[0][k][m : m + 1, :] for k in range(8)] for m in range(8)]
        rows, inverses = [], []
        final = None
        for k in range(8):
            factors = [pivots[m][k] * inverses[m] for m in range(k)]
            for c in range(k, 8):
                for m in range(k):
                    pivots[k][c] -= factors[m] * pivots[m][c]
            inverses.append(1.0 / pivots[k][k])
            unit = jnp.where(lane == j + k, 1.0, 0.0)
            row = jnp.where((lane >= j) & (lane < j + 8), unit, tiles[t][k : k + 1, :])
            for m in range(k):
                row -= factors[m] * rows[m]
            rows.append(row)
            scaled = jnp.where(lane <= j + k, row, 0.0) * lax.rsqrt(pivots[k][k])
            scaled = jnp.broadcast_to(scaled, (8, TILE))
            final = scaled if k == 0 else jnp.where(sublane == k, scaled, final)
        out.append(final)
        for i in range(t + 1, groups):
            factors = []
            new = jnp.where((lanes >= j) & (lanes < j + 8), 0.0, tiles[i])
            for k in range(8):
                value = columns[i - t][k]
                for m in range(k):
                    value -= factors[m] * pivots[m][k]
                factors.append(value * inverses[k])
                new -= factors[k] * rows[k]
            tiles[i] = new
    return jnp.concatenate(out, axis=0)


def exact_dot(left, right, contract):
    return lax.dot_general(
        left,
        right,
        (contract, ((), ())),
        precision=HIGHEST,
        preferred_element_type=jnp.float32,
    )


def factor_kernel(pivot_ref, out_ref, work):
    work[...] = pivot_ref[...]
    for k in range(PANEL // TILE):
        low, high = k * TILE, (k + 1) * TILE
        inverse = eliminate(work[low:high, low:high])
        work[low:high, low:high] = inverse
        if k > 0:
            work[low:high, :low] = exact_dot(inverse, work[low:high, :low], ((1,), (0,)))
        if high < PANEL:
            right = exact_dot(inverse, work[low:high, high:], ((1,), (0,)))
            work[low:high, high:] = right
            work[high:, low:high] = jnp.zeros((PANEL - high, TILE), jnp.float32)
            work[high:, :] -= exact_dot(right, work[low:high, :], ((0,), (0,)))
            work[low:high, high:] = jnp.zeros_like(right)
    out_ref[...] = work[...]


def inverse_factor(pivot_block):
    return pl.pallas_call(
        factor_kernel,
        out_shape=jax.ShapeDtypeStruct((PANEL, PANEL), jnp.float32),
        in_specs=[pl.BlockSpec(memory_space=pltpu.VMEM)],
        out_specs=pl.BlockSpec(memory_space=pltpu.VMEM),
        scratch_shapes=[pltpu.VMEM((PANEL, PANEL), jnp.float32)],
        compiler_params=pltpu.CompilerParams(vmem_limit_bytes=24 * 2**20),
        cost_estimate=pl.CostEstimate(
            flops=300_000_000, bytes_accessed=2 * 2**20, transcendentals=0
        ),
        name="inverse_factor",
    )(pivot_block)


def split(value):
    high = value.astype(jnp.bfloat16)
    return high, (value - high.astype(jnp.float32)).astype(jnp.bfloat16)


def split_dot(left, right, contract):
    def dot(a, b):
        return lax.dot_general(a, b, (contract, ((), ())), preferred_element_type=jnp.float32)

    return dot(left[0], right[0]) + (dot(left[0], right[1]) + dot(left[1], right[0]))


def solve_kernel(inverse_ref, top_ref, rows_ref, lower_ref, upper_ref):
    inverse = split(inverse_ref[...])
    for j in range(8):
        lower_ref[TILE * j : TILE * (j + 1), :] = split_dot(
            split(rows_ref[j]), inverse, ((0,), (1,))
        )
    wide = 256
    for j in range(0, top_ref.shape[1], wide):
        upper_ref[:, j : j + wide] = split_dot(
            inverse, split(top_ref[:, j : j + wide]), ((1,), (0,))
        )


def solve(inverse, panel_top, row_panel):
    vmem = pl.BlockSpec(memory_space=pltpu.VMEM)
    return pl.pallas_call(
        solve_kernel,
        out_shape=(
            jax.ShapeDtypeStruct((PIECES * PIECE, PANEL), jnp.float32),
            jax.ShapeDtypeStruct(panel_top.shape, jnp.float32),
        ),
        in_specs=[vmem] * 3,
        out_specs=(vmem, vmem),
        compiler_params=pltpu.CompilerParams(vmem_limit_bytes=40 * 2**20),
        cost_estimate=pl.CostEstimate(
            flops=3_000_000_000, bytes_accessed=9 * 2**20, transcendentals=0
        ),
        name="solve",
    )(inverse, panel_top, row_panel)


def extend_add_kernel(place_ref, map_ref, parent_ref, *refs):
    pieces, out_ref = refs[:PIECES], refs[PIECES]
    my_front, my_row, my_col = place_ref[0], place_ref[1], place_ref[2]
    local_row, group = pl.program_id(0), pl.program_id(1)
    col_tiles = pieces[0].shape[1] // TILE
    pivot_tiles = PANEL // TILE

    def bit(front, tile):
        found = map_ref[front, jnp.maximum(tile - pivot_tiles, 0)] - 2 * tile
        return jnp.where(tile >= pivot_tiles, found, -1)

    row_tile = 2 * (8 * my_front + my_row) + local_row
    fronts = [my_front ^ (my_row & 3) ^ k for k in range(PIECES)]
    row_bits = [bit(front, row_tile) for front in fronts]
    for u in range(col_tiles):
        col_tile = 8 * my_col + group * col_tiles + u
        col_bits = [bit(front, col_tile) for front in fronts]
        blocks = [piece[:, u * TILE : (u + 1) * TILE] for piece in pieces]
        for a in range(2):
            for b in range(2):
                rows = slice(a * TILE, (a + 1) * TILE)
                columns = slice((2 * u + b) * TILE, (2 * u + b + 1) * TILE)
                total = parent_ref[rows, columns]
                for k in range(PIECES):
                    hit = jnp.logical_and(row_bits[k] == a, col_bits[k] == b)
                    total += jnp.where(hit, blocks[k], 0.0)
                out_ref[rows, columns] = total


def extend_add(place, child_map, parent, pieces):
    groups = 2
    rows, columns = pieces[0].shape
    wide = columns // groups
    piece_spec = pl.BlockSpec((TILE, wide), lambda i, g, *_: (i, g))
    parent_spec = pl.BlockSpec((2 * TILE, 2 * wide), lambda i, g, *_: (i, g))
    return pl.pallas_call(
        extend_add_kernel,
        out_shape=jax.ShapeDtypeStruct(parent.shape, jnp.float32),
        grid_spec=pltpu.PrefetchScalarGridSpec(
            num_scalar_prefetch=2,
            grid=(rows // TILE, groups),
            in_specs=[parent_spec] + [piece_spec] * PIECES,
            out_specs=parent_spec,
        ),
        cost_estimate=pl.CostEstimate(
            flops=8 * 2**20, bytes_accessed=12 * 2**20, transcendentals=0
        ),
        name="extend_add",
    )(place, child_map, parent, *pieces)


def fan_out(parts, axis, numbers):
    received = [lax.ppermute(parts[k], axis, [numbers(k)]) for k in range(1, 8)]
    return functools.reduce(jnp.add, received)


def local(front_block, child_map, parent_entries):
    matrix = front_block[0]
    my_front = lax.axis_index("front")
    my_row = lax.axis_index("row")
    my_col = lax.axis_index("col")
    quarter = my_row & 3
    chunk = PANEL // 8

    place = jnp.stack([my_front, my_row, my_col]).astype(jnp.int32)

    with jax.named_scope("pivot_to_columns"):
        parts = [matrix[chunk * k : chunk * (k + 1), :PANEL] for k in range(8)]
        part = fan_out(parts, PLANE_AXES, lambda k: (0, k))
        part = jnp.where(my_col == 0, parts[0], part)

    with jax.named_scope("panel_scatter"):
        parts = [matrix[chunk * k : chunk * (k + 1), :] for k in range(8)]
        panel_part = fan_out(parts, "row", lambda k: (0, k))
        panel_part = jnp.where(my_row == 0, parts[0], panel_part)

    with jax.named_scope("pivot_along_z"):
        for distance in (4, 2, 1):
            pairs = [(r, r + distance) for r in range(0, 8, 2 * distance)]
            far = lax.ppermute(part, "row", pairs)
            part = jnp.where((my_row & (2 * distance - 1)) == distance, far, part)

    with jax.named_scope("pivot_in_plane"):
        pivot_block = lax.all_gather(part, "col", tiled=True)

    with jax.named_scope("panel_gather"):
        panel_top = lax.all_gather(panel_part, "row", tiled=True)

    with jax.named_scope("rows_along_z"):
        pieces = [(my_row // 2) ^ k ^ my_front for k in range(PIECES)]
        sent = [lax.dynamic_slice_in_dim(matrix, piece * PIECE, PIECE, 0) for piece in pieces]
        panel_top, *sent = lax.optimization_barrier((panel_top, *sent))
        arrived = []
        for k in range(PIECES):
            pairs = [
                (f * 8 + r, f * 8 + 4 * (r % 2) + ((r // 2) ^ k ^ f))
                for f in range(4)
                for r in range(8)
            ]
            arrived.append(lax.ppermute(sent[k], FRONT_AXES, pairs))

    with jax.named_scope("row_panel"):
        half = my_col & 1
        start = PIECE * quarter
        mine = lax.dynamic_slice_in_dim(panel_top, start + TILE * half, TILE, 1)
        other = lax.dynamic_slice_in_dim(panel_top, start + TILE * (1 - half), TILE, 1)
        pairs = [
            (r * 8 + 2 * y + r // 4, r * 8 + 2 * y + 1 - r // 4) for r in range(8) for y in range(4)
        ]
        other = lax.ppermute(other, PLANE_AXES, pairs)
        mine = jnp.where(half == my_row // 4, mine, other)
        row_panel = lax.all_gather(mine, "col")

    with jax.named_scope("factor"):
        inverse = inverse_factor(pivot_block)

    with jax.named_scope("solve"):
        lower, upper = solve(inverse, panel_top, row_panel)

    pieces = []
    for k in range(PIECES):
        with jax.named_scope("schur"):
            target = quarter ^ k ^ my_front
            left = lax.dynamic_slice_in_dim(lower, target * PIECE, PIECE, 0)
            schur = arrived[k] - jnp.dot(
                left, upper, precision=HIGH, preferred_element_type=jnp.float32
            )
        with jax.named_scope("to_parent"):
            pairs = [(f * 8 + r, (f ^ (r & 3) ^ k) * 8 + r) for f in range(4) for r in range(8)]
            pieces.append(lax.ppermute(schur, FRONT_AXES, pairs))

    with jax.named_scope("extend_add"):
        return extend_add(place, child_map, parent_entries, pieces)


def solution(mesh):
    in_specs = (P("front", "row", "col"), P(), P(("front", "row"), "col"))
    out_specs = P(("front", "row"), "col")
    return jax.shard_map(local, mesh=mesh, in_specs=in_specs, out_specs=out_specs, check_vma=False)
```
